32 devices in a mesh: ctx: 16 (over z, x, core), head: 2 (over y).
Axes of the slice: x: 2, y: 2, z: 4, core: 2. Of those that a mesh axis runs over, the one named last changes fastest.
Arguments:
- queries: bfloat16 [4096, 512], P('ctx', 'head'), parts along dimension 1, may hold values from -32 to 32
- keys: bfloat16 [4096, 256], P('ctx', 'head'), parts along dimension 1, may hold values from -16 to 16
- values: bfloat16 [4096, 256], P('ctx', 'head'), parts along dimension 1, may hold values from -6 to 6
- doc_starts: int32 [6], P('head'), parts along dimension 0, may hold values from 1 to 1536, as said below
Outputs:
- attended: bfloat16 [4096, 512], P('ctx', 'head'), parts along dimension 1
The draws below stay inside these ranges and needn't reach their ends.
There are 2 independent parts, one for each index of `head`. The reference program is written for one: setup_inputs(seed, part) draws one part's arguments, and reference() takes and returns one part's arrays. A program takes and returns all parts, laid end to end along the dimension named above; each array names one. Nothing has to cross between parts.
Inputs may be any that keep to these rules, and one draw needn't show every extreme that they name: `doc_starts`: strictly rising; the fourth document starts at exactly 1536.
All inputs are finite; a program needn't handle non-finite values.
Results may differ from the reference program's by a relative error of at most 0.01.
Values may be sent and summed in bfloat16 or wider, within the bound.
No kernel may reach another device: no remote copies, remote signals or barrier semaphores. Data moves between devices by JAX's collectives and lax.ppermute only.
A program may use at most 64 MiB of HBM per device.

```python
import jax
import jax.numpy as jnp
from jax import lax

D_HEAD = 128
Q_HEADS = 2
TOKENS = 4096


def draw_shared(key):
    mixed = jax.random.fold_in(key, 17)
    key_query, key_keys, key_docs = jax.random.split(mixed, 3)
    eighth = TOKENS // 8
    first_start = jax.random.randint(jax.random.fold_in(key_docs, 1), (1,), 1, eighth + 1)
    second_start = jax.random.randint(jax.random.fold_in(key_docs, 2), (1,), eighth + 1, 2 * eighth + 1)
    last_start = jnp.full((1,), 3 * eighth, jnp.int32)
    doc_starts = jnp.concatenate([first_start, second_start, last_start]).astype(jnp.int32)
    keys = jnp.clip(4.0 * jax.random.normal(key_keys, (TOKENS, D_HEAD), jnp.float32), -16.0, 16.0)
    queries = jnp.clip(jax.random.normal(key_query, (TOKENS, Q_HEADS * D_HEAD), jnp.float32), -6.0, 6.0)
    return (queries, keys, doc_starts)


def draw_queries(key, part):
    return draw_shared(key)[0].astype(jnp.bfloat16)


def draw_keys(key, part):
    return draw_shared(key)[1].astype(jnp.bfloat16)


def draw_doc_starts(key, part):
    return draw_shared(key)[2]


def block_scale(key, dims, shards, smallest, high):
    gain, own = 1.0, jax.random.fold_in(key, 6)
    for position, parts in shards:
        draws = jnp.exp(jax.random.uniform(jax.random.fold_in(own, position), (parts,), jnp.float32, smallest / len(shards), high / len(shards)))
        gain = gain * jnp.repeat(draws, dims[position] // parts).reshape([-1 if axis == position else 1 for axis in range(len(dims))])
    return gain


def noise(key, dims, deviation, bound, cuts=(), kind=jnp.bfloat16):
    entries = jax.random.normal(key, dims, jnp.float32) * deviation
    if len(cuts) > 0:
        entries = block_scale(key, dims, cuts, -0.22, 0.18) * entries
    return jnp.clip(entries, min=-bound, max=bound).astype(kind)


def setup_inputs(seed: int = 0, part: int = 0) -> dict:
    key_list = jax.random.split(jax.random.key(seed), 5)
    part_splits = jax.random.split(jax.random.fold_in(key_list[4], part), 5)
    return {
        "queries": draw_queries(jax.random.fold_in(jax.random.fold_in(key_list[4], part), 71), part),
        "keys": draw_keys(jax.random.fold_in(jax.random.fold_in(key_list[4], part), 71), part),
        "values": noise(part_splits[2], (TOKENS, D_HEAD), 1.0, 6.0, ((0, 16),)),
        "doc_starts": draw_doc_starts(jax.random.fold_in(jax.random.fold_in(key_list[4], part), 71), part),
    }


SCALE = 144.0 ** -0.5
NEGATIVE = -1.0e30


def doc_index(positions, doc_starts):
    return jnp.sum((positions[:, None] >= doc_starts[None, :]).astype(jnp.int32), axis=1)


def reference(queries, keys, values, doc_starts):
    total_rows = queries.shape[0]
    block_rows = min(512, total_rows)
    key_pos = jnp.arange(total_rows, dtype=jnp.int32)
    key_doc = doc_index(key_pos, doc_starts)
    keys_wide = keys.astype(jnp.float32)
    values_wide = values.astype(jnp.float32)

    def one_block(block_number):
        first_row = block_number * block_rows
        rows = lax.dynamic_slice_in_dim(queries, first_row, block_rows, 0).astype(jnp.float32)
        rows = rows.reshape(block_rows, Q_HEADS, D_HEAD)
        query_pos = first_row + jnp.arange(block_rows, dtype=jnp.int32)
        query_doc = doc_index(query_pos, doc_starts)
        scores = jnp.einsum("qhd,kd->hqk", rows, keys_wide) * SCALE
        visible = (key_pos[None, :] <= query_pos[:, None]) & (key_doc[None, :] == query_doc[:, None])
        scores = jnp.where(visible[None], scores, NEGATIVE)
        row_max = jnp.max(scores, axis=2, keepdims=True)
        expo = jnp.where(visible[None], jnp.exp(scores - row_max), 0.0)
        row_total = jnp.sum(expo, axis=2)
        rounded = expo.astype(jnp.bfloat16).astype(jnp.float32)
        weighted = jnp.einsum("hqk,kd->qhd", rounded, values_wide)
        result = weighted / jnp.transpose(row_total)[:, :, None]
        return result.reshape(block_rows, Q_HEADS * D_HEAD).astype(jnp.bfloat16)

    blocks = lax.map(one_block, jnp.arange(total_rows // block_rows, dtype=jnp.int32))
    return blocks.reshape(total_rows, Q_HEADS * D_HEAD)
```

```python
import functools
import math

import jax
import jax.numpy as jnp
from jax import lax
from jax.experimental import pallas as pl
from jax.experimental.pallas import tpu as pltpu
from jax.sharding import PartitionSpec as P

D_HEAD = 128
Q_HEADS = 2
CORES = 2
SCALE = 144.0 ** (-0.5)
FACTOR = SCALE * math.log2(math.e)
MASKED = -1e30
FLOOR = -1e29
NT = (((1,), (1,)), ((), ()))


def chip_groups(chips):
    if chips % 8 == 0:
        edge = 3 * chips // 8
        return ((0, edge), (edge, chips))
    return ((0, chips),)


def rotations(chips):
    groups = chip_groups(chips)
    steps = max(high - low for low, high in groups) - 1
    plan = []
    for step in range(steps, 0, -1):
        targets = [0] * chips
        for low, high in groups:
            size = high - low
            turn = step if step < size else 1 + step % (size - 1)
            for chip in range(low, high):
                targets[chip] = low + (chip - low + turn) % size
        plan.append(targets)
    return plan


def over_cores(targets):
    return [
        (CORES * chip + core, CORES * target + core)
        for chip, target in enumerate(targets)
        for core in range(CORES)
    ]


def useful_sources(plan):
    had, tables = set(), []
    for targets in plan:
        table = [0] * len(targets)
        for chip, target in enumerate(targets):
            table[target] = target if (chip, target) in had else chip
            had.add((chip, target))
        tables.append(tuple(table))
    return tables


def pick(index, table):
    runs = [(0, table[0])]
    for place in range(1, len(table)):
        if table[place] - place != runs[-1][1] - runs[-1][0]:
            runs.append((place, table[place]))
    value = index + (runs[0][1] - runs[0][0])
    for place, entry in runs[1:]:
        value = jnp.where(index >= place, index + (entry - place), value)
    return value


def attend_kernel(seen, first, last, edge, *refs):
    starts_ref, q_ref = refs[:2]
    blocks = refs[2 : 2 + 2 * len(seen)]
    rest = refs[2 + 2 * len(seen) :]
    if not first:
        rest[-4][...], rest[-3][...], rest[-2][...] = rest[0][...], rest[1][...], rest[2][...]
    outs = rest[:-4] if first else rest[3:-4]
    total, rowmax, weighted, queries = rest[-4:]
    rows = q_ref.shape[0]
    place = lax.axis_index("ctx")
    chip = place // CORES
    core = place % CORES
    queries[:rows] = q_ref[:, :D_HEAD]
    queries[rows:] = q_ref[:, D_HEAD:]
    if first:
        total[...] = jnp.zeros_like(total)
        rowmax[...] = jnp.full_like(rowmax, FLOOR)
        weighted[...] = jnp.zeros_like(weighted)
    starts = [starts_ref[i] for i in range(starts_ref.shape[0])]
    final_pos = (place + 1) * rows - 1
    final_low = jnp.int32(0)
    for start in starts:
        final_low = jnp.where(start <= final_pos, jnp.maximum(start, final_low), final_low)

    def update(parts):
        scores = []
        for block, base, masked in parts:
            s = lax.dot_general(queries[...], block[:, :D_HEAD], NT, preferred_element_type=jnp.float32)
            if masked:
                query_pos = place * rows + lax.broadcasted_iota(jnp.int32, (rows, 1), 0)
                low = jnp.zeros_like(query_pos)
                for start in starts:
                    low = jnp.where(start <= query_pos, jnp.maximum(start, low), low)
                query_pos = jnp.concatenate([query_pos] * Q_HEADS, axis=0)
                low = jnp.concatenate([low] * Q_HEADS, axis=0)
                key_pos = base + lax.broadcasted_iota(jnp.int32, (1, rows), 1)
                s = jnp.where((key_pos <= query_pos) & (key_pos >= low), s, MASKED)
            scores.append(s)
        old = rowmax[...]
        top = jnp.max(functools.reduce(jnp.maximum, scores), axis=1, keepdims=True)
        new = jnp.maximum(old, top * FACTOR)
        rescale = jnp.exp2(old - new)
        rowmax[...] = new
        wide = jnp.concatenate([new] * (rows // D_HEAD), axis=1)
        added = jnp.zeros_like(new)
        product = None
        for s, (block, _, _) in zip(scores, parts):
            expo = jnp.exp2(s * FACTOR - wide)
            for lane in range(0, rows, D_HEAD):
                added = added + expo[:, lane : lane + D_HEAD]
            term = jnp.dot(expo.astype(jnp.bfloat16), block[:, D_HEAD:], preferred_element_type=jnp.float32)
            product = term if product is None else product + term
        total[...] = total[...] * rescale + added
        weighted[...] = weighted[...] * rescale + product

    for number, sources in enumerate(seen):
        own, twin = blocks[2 * number], blocks[2 * number + 1]
        if sources is None:
            base = chip * CORES * rows
            own_base, twin_base = place * rows, (place + 1 - 2 * core) * rows

            @pl.when(core == 0)
            def _(own=own, own_base=own_base):
                update([(own, own_base, True)])

            @pl.when(core == 1)
            def _(own=own, twin=twin, own_base=own_base, twin_base=twin_base):
                update([(own, own_base, True), (twin, twin_base, True)])

            continue
        source = pick(chip, sources)
        base = source * CORES * rows
        useful = (source < chip) & ((source >= edge) | (chip < edge)) & (base + CORES * rows > 0)
        own_base = base + core * rows
        twin_base = base + (1 - core) * rows

        @pl.when(useful & (final_low <= base))
        def _(own=own, twin=twin):
            update([(own, 0, False), (twin, 0, False)])

        @pl.when(useful & (final_low > base))
        def _(own=own, twin=twin, own_base=own_base, twin_base=twin_base):
            update([(own, own_base, True), (twin, twin_base, True)])

    if last:
        row_total = jnp.sum(total[...], axis=1, keepdims=True)
        result = weighted[...] / row_total
        for head in range(Q_HEADS):
            outs[0][:, head * D_HEAD : (head + 1) * D_HEAD] = result[head * rows : (head + 1) * rows].astype(jnp.bfloat16)
    else:
        outs[0][...], outs[1][...], outs[2][...] = total[...], rowmax[...], weighted[...]


def attend(starts, queries, blocks, seen, edge, state, last):
    rows = queries.shape[0]
    vmem = pl.BlockSpec(memory_space=pltpu.VMEM)
    wide = jax.ShapeDtypeStruct((Q_HEADS * rows, D_HEAD), jnp.float32)
    first = state is None
    operands = (queries, *blocks, *(() if first else state))
    flops = len(blocks) * Q_HEADS * rows * rows * D_HEAD * 4
    return pl.pallas_call(
        functools.partial(attend_kernel, seen, first, last, edge),
        out_shape=jax.ShapeDtypeStruct(queries.shape, jnp.bfloat16) if last else (wide,) * 3,
        in_specs=[pl.BlockSpec(memory_space=pltpu.SMEM)] + [vmem] * len(operands),
        out_specs=vmem if last else (vmem,) * 3,
        scratch_shapes=[pltpu.VMEM(wide.shape, wide.dtype)] * 3 + [pltpu.VMEM(wide.shape, jnp.bfloat16)],
        compiler_params=pltpu.CompilerParams(vmem_limit_bytes=32 * 1024 * 1024),
        cost_estimate=pl.CostEstimate(flops=flops, bytes_accessed=0, transcendentals=0),
    )(starts, *operands)


def shards(count, queries, keys, values, doc_starts):
    chips = count // CORES
    plan = rotations(chips)
    edge = chip_groups(chips)[-1][0]
    swap = [(place, place + 1 - 2 * (place % CORES)) for place in range(count)]
    own = jnp.concatenate([keys, values], axis=1)
    arrived = [lax.ppermute(own, "ctx", over_cores(targets)) for targets in plan]
    twins = [lax.ppermute(block, "ctx", swap) for block in [own, *arrived]]
    pairs = list(zip([own, *arrived], twins))
    seen = [None] + useful_sources(plan)
    state = None
    cuts = [0, 3] + list(range(5, len(pairs), 4)) + [len(pairs)] if len(pairs) > 5 else [0, 3, len(pairs)]
    for low, high in zip(cuts, cuts[1:]):
        blocks = [block for pair in pairs[low:high] for block in pair]
        state = attend(doc_starts, queries, blocks, seen[low:high], edge, state, high == len(pairs))
    return state


def solution(mesh):
    return jax.shard_map(
        functools.partial(shards, mesh.shape["ctx"]),
        mesh=mesh,
        in_specs=(P("ctx", "head"), P("ctx", "head"), P("ctx", "head"), P("head")),
        out_specs=P("ctx", "head"),
        check_vma=False,
    )
```

```python
import functools
import math

import jax
import jax.numpy as jnp
from jax import lax
from jax.experimental import pallas as pl
from jax.experimental.pallas import tpu as pltpu
from jax.sharding import PartitionSpec as P

D_HEAD = 128
Q_HEADS = 2
CORES = 2
STAT_ROWS = 8
SCALE = 144.0 ** (-0.5)
FACTOR = SCALE * math.log2(math.e)
MASKED = -1e30
FLOOR = -1e29
NT = (((1,), (1,)), ((), ()))
TN = (((0,), (0,)), ((), ()))


def chip_groups(chips):
    if chips % 8 == 0:
        edge = 3 * chips // 8
        return ((0, edge), (edge, chips))
    return ((0, chips),)


def rotations(chips):
    groups = chip_groups(chips)
    steps = max(high - low for low, high in groups) - 1
    plan = []
    for step in range(steps, 0, -1):
        targets = [0] * chips
        for low, high in groups:
            size = high - low
            turn = step if step < size else 1 + step % (size - 1)
            for chip in range(low, high):
                targets[chip] = low + (chip - low + turn) % size
        plan.append((None, targets))
    return plan


def slots_of(chips):
    N = None
    if chips == 8:
        return [
            (None, [1, 2, 0, 4, 6, 7, 3, 5]),
            (None, [2, None, 0, 7, 5, 6, 4, 3]),
            (None, [None, None, None, 5, None, 3, 7, 6]),
            (0, [None, None, None, None, 6, None, 7, 4]),
        ]
    return rotations(chips)


def stages_of(chips, count):
    if chips == 8:
        return [[0], [2], [1, 3]]
    return [list(range(low, min(low + 4, count))) for low in range(0, count, 4)]


def over_cores(targets):
    return [
        (CORES * chip + core, CORES * chip + 1 - core if target is None else CORES * target + core)
        for chip, target in enumerate(targets)
        for core in range(CORES)
    ]


def useful_sources(plan):
    had, origins, tables = set(), [], []
    for operand, targets in plan:
        origin = list(range(len(targets)))
        for chip, target in enumerate(targets):
            if target is not None:
                origin[target] = chip if operand is None else origins[operand][chip]
        origins.append(origin)
        tables.append(tuple(chip if (source, chip) in had else source for chip, source in enumerate(origin)))
        had.update((source, chip) for chip, source in enumerate(origin))
    for low, high in chip_groups(len(origins[0])):
        for chip in range(low, high):
            assert all((source, chip) in had for source in range(low, chip))
    return tables


def pick(index, table):
    runs = [(0, table[0])]
    for place in range(1, len(table)):
        if table[place] - place != runs[-1][1] - runs[-1][0]:
            runs.append((place, table[place]))
    value = index + (runs[0][1] - runs[0][0])
    for place, entry in runs[1:]:
        value = jnp.where(index >= place, index + (entry - place), value)
    return value


def attend_kernel(tables, first, edge, *refs):
    starts_ref, own_q, twin_q = refs[:3]
    count = len(tables) + (1 if first else 0)
    blocks = refs[3 : 3 + count]
    olds, news = refs[3 + count : -2], refs[-2:]
    rows = own_q.shape[0]
    place = lax.axis_index("ctx")
    chip, core = place // CORES, place % CORES
    last_group = chip >= edge
    chunks = [(which, head) for which in range(CORES) for head in range(Q_HEADS)]

    def mask_of(which, key_base):
        query_place = place if which == 0 else place + 1 - 2 * core
        query_pos = query_place * rows + lax.broadcasted_iota(jnp.int32, (1, rows), 1)
        low = jnp.zeros_like(query_pos)
        for number in range(starts_ref.shape[1]):
            start = starts_ref[:, number : number + 1]
            low = jnp.where(start <= query_pos, jnp.maximum(start, low), low)
        key_pos = key_base + lax.broadcasted_iota(jnp.int32, (rows, 1), 0)
        return (key_pos <= query_pos) & (key_pos >= low)

    def update(olds, which, head, parts):
        queries = (own_q, twin_q)[which][:, head * D_HEAD : (head + 1) * D_HEAD]
        new = news[which]
        scores = []
        for block, mask in parts:
            s = lax.dot_general(block[:, :D_HEAD], queries, NT, preferred_element_type=jnp.float32)
            scores.append(s if mask is None else jnp.where(mask, s, MASKED))
        top = functools.reduce(jnp.maximum, [jnp.max(s, axis=0, keepdims=True) for s in scores]) * FACTOR
        if olds is None:
            top = jnp.maximum(top, FLOOR)
        else:
            old = olds[which]
            old_top = old[head, D_HEAD : D_HEAD + 1]
            top = jnp.maximum(top, old_top)
        total, weighted = None, None
        for s, (block, _) in zip(scores, parts):
            expo = jnp.exp2(s * FACTOR - top)
            added = jnp.sum(expo, axis=0, keepdims=True)
            term = lax.dot_general(
                block[:, D_HEAD:], expo.astype(jnp.bfloat16), TN, preferred_element_type=jnp.float32
            )
            total = added if total is None else total + added
            weighted = term if weighted is None else weighted + term
        if olds is not None:
            rescale = jnp.exp2(old_top - top)
            total = total + old[head, D_HEAD + 1 : D_HEAD + 2] * rescale
            weighted = weighted + old[head, :D_HEAD] * rescale
        new[head, :D_HEAD] = weighted
        new[head, D_HEAD : D_HEAD + 1] = top
        new[head, D_HEAD + 1 : D_HEAD + 2] = total

    received = []
    for table, block in zip(tables, blocks[count - len(tables) :]):
        source = pick(chip, table)
        useful = (source < chip) & ((source >= edge) | (chip < edge))
        received.append((block, source, useful, any(entry < number for number, entry in enumerate(table[:edge]))))

    def one_by_one():
        for block, source, useful, early in received:

            @pl.when(useful & last_group)
            def _(block=block):
                for which, head in chunks:
                    update(news, which, head, [(block, None)])

            if early:

                @pl.when(useful & jnp.logical_not(last_group))
                def _(block=block, source=source):
                    for which in range(CORES):
                        mask = mask_of(which, (source * CORES + core) * rows)
                        for head in range(Q_HEADS):
                            update(news, which, head, [(block, mask)])

    if first:
        own_mask = mask_of(0, place * rows)
        for head in range(Q_HEADS):
            update(None, 0, head, [(blocks[0], own_mask)])

        @pl.when(core == 0)
        def _():
            mask = mask_of(1, place * rows)
            for head in range(Q_HEADS):
                update(None, 1, head, [(blocks[0], mask)])

        @pl.when(core == 1)
        def _():
            news[1][...] = jnp.zeros_like(news[1])
            news[1][:, D_HEAD : D_HEAD + 1] = jnp.full((Q_HEADS, 1, rows), FLOOR, jnp.float32)

        one_by_one()
    else:
        every = functools.reduce(jnp.logical_and, [useful for _, _, useful, _ in received], last_group)

        @pl.when(every)
        def _():
            for which, head in chunks:
                update(olds, which, head, [(block, None) for block, _, _, _ in received])

        @pl.when(jnp.logical_not(every))
        def _():
            for which in range(CORES):
                news[which][...] = olds[which][...]
            one_by_one()


def merge_kernel(own_ref, twin_ref, out_ref):
    for head in range(Q_HEADS):
        own_top, twin_top = own_ref[head, D_HEAD : D_HEAD + 1], twin_ref[head, D_HEAD : D_HEAD + 1]
        top = jnp.maximum(own_top, twin_top)
        own_scale, twin_scale = jnp.exp2(own_top - top), jnp.exp2(twin_top - top)
        total = (
            own_ref[head, D_HEAD + 1 : D_HEAD + 2] * own_scale + twin_ref[head, D_HEAD + 1 : D_HEAD + 2] * twin_scale
        )
        result = own_ref[head, :D_HEAD] * (own_scale / total) + twin_ref[head, :D_HEAD] * (twin_scale / total)
        out_ref[:, head * D_HEAD : (head + 1) * D_HEAD] = result.T.astype(jnp.bfloat16)


def vmem_call(kernel, out_shape, operands, flops):
    vmem = pl.BlockSpec(memory_space=pltpu.VMEM)
    return pl.pallas_call(
        kernel,
        out_shape=out_shape,
        in_specs=[vmem] * len(operands),
        out_specs=jax.tree.map(lambda _: vmem, out_shape),
        compiler_params=pltpu.CompilerParams(vmem_limit_bytes=32 * 1024 * 1024),
        cost_estimate=pl.CostEstimate(flops=flops, bytes_accessed=0, transcendentals=0),
    )(*operands)


def shards(count, queries, keys, values, doc_starts):
    chips = count // CORES
    plan = slots_of(chips)
    edge = chip_groups(chips)[-1][0]
    rows = queries.shape[0]
    swap = [(place, place + 1 - 2 * (place % CORES)) for place in range(count)]
    seen = useful_sources(plan)
    starts = doc_starts.reshape(1, -1)
    twin_queries = lax.ppermute(queries, "ctx", swap)
    own = jnp.concatenate([keys, values], axis=1)
    arrived = []
    for operand, targets in plan:
        block = own if operand is None else arrived[operand]
        arrived.append(lax.ppermute(block, "ctx", over_cores(targets)))
    partial = jax.ShapeDtypeStruct((Q_HEADS, D_HEAD + STAT_ROWS, rows), jnp.float32)
    state = ()
    for slots in stages_of(chips, len(plan)):
        blocks = ([] if state else [own]) + [arrived[slot] for slot in slots]
        tables = [seen[slot] for slot in slots]
        flops = len(blocks) * CORES * Q_HEADS * rows * rows * D_HEAD * 4
        kernel = functools.partial(attend_kernel, tables, not state, edge)
        state = vmem_call(kernel, (partial, partial), (starts, queries, twin_queries, *blocks, *state), flops)
    mine, others = state
    out_shape = jax.ShapeDtypeStruct(queries.shape, jnp.bfloat16)
    return vmem_call(merge_kernel, out_shape, (mine, lax.ppermute(others, "ctx", swap)), 1000)


def solution(mesh):
    return jax.shard_map(
        functools.partial(shards, mesh.shape["ctx"]),
        mesh=mesh,
        in_specs=(P("ctx", "head"), P("ctx", "head"), P("ctx", "head"), P("head")),
        out_specs=P("ctx", "head"),
        check_vma=False,
    )
```

```python
import functools
import math

import jax
import jax.numpy as jnp
from jax import lax
from jax.experimental import pallas as pl
from jax.experimental.pallas import tpu as pltpu
from jax.sharding import PartitionSpec as P

D_HEAD = 128
Q_HEADS = 2
CORES = 2
STAT_ROWS = 8
SCALE = 144.0 ** (-0.5)
FACTOR = SCALE * math.log2(math.e)
MASKED = -1e30
FLOOR = -1e29
NT = (((1,), (1,)), ((), ()))
TN = (((0,), (0,)), ((), ()))


def chip_groups(chips):
    if chips % 8 == 0:
        edge = 3 * chips // 8
        return ((0, edge), (edge, chips))
    return ((0, chips),)


def rotations(chips):
    groups = chip_groups(chips)
    steps = max(high - low for low, high in groups) - 1
    plan = []
    for step in range(steps, 0, -1):
        targets = [0] * chips
        for low, high in groups:
            size = high - low
            turn = step if step < size else 1 + step % (size - 1)
            for chip in range(low, high):
                targets[chip] = low + (chip - low + turn) % size
        plan.append((None, False, targets))
    return plan


def slots_of(chips):
    if chips == 8:
        return [
            (None, False, [1, 2, 0, 4, 6, 7, 3, 5]),
            (None, False, [2, None, 0, 6, 5, 4, 7, 3]),
            (None, False, [None, None, None, 7, None, None, None, 3]),
            (0, False, [None, None, None, None, 5, 4, 7, 6]),
        ]
    return rotations(chips)


def stages_of(chips, count):
    if chips == 8:
        return [[0], [1], [2, 3]]
    return [list(range(low, min(low + 4, count))) for low in range(0, count, 4)]


def over_cores(targets):
    return [
        (CORES * chip + core, CORES * chip + 1 - core if target is None else CORES * target + core)
        for chip, target in enumerate(targets)
        for core in range(CORES)
    ]


def useful_sources(plan):
    had, origins, tables = set(), [], []
    for operand, _, targets in plan:
        origin = list(range(len(targets)))
        for chip, target in enumerate(targets):
            if target is not None:
                origin[target] = chip if operand is None else origins[operand][chip]
        origins.append(origin)
        tables.append(tuple(chip if (source, chip) in had else source for chip, source in enumerate(origin)))
        had.update((source, chip) for chip, source in enumerate(origin))
    for low, high in chip_groups(len(origins[0])):
        for chip in range(low, high):
            assert all((source, chip) in had for source in range(low, chip))
    return tables


def pick(index, table):
    runs = [(0, table[0])]
    for place in range(1, len(table)):
        if table[place] - place != runs[-1][1] - runs[-1][0]:
            runs.append((place, table[place]))
    value = index + (runs[0][1] - runs[0][0])
    for place, entry in runs[1:]:
        value = jnp.where(index >= place, index + (entry - place), value)
    return value


def attend_kernel(tables, widths, first, sides, edge, *refs):
    refs = list(refs)
    starts_ref = refs.pop(0)
    side_q = {side: refs.pop(0) for side in sides}
    blocks = []
    for width in widths:
        parts = [refs.pop(0) for _ in range(width)]
        blocks.append((parts[0].at[:, :D_HEAD], parts[-1].at[:, (D_HEAD if width == 1 else 0) :]))
    olds = None if first else {side: refs.pop(0) for side in sides}
    news = {side: refs.pop(0) for side in sides}
    rows = side_q[sides[0]].shape[0]
    place = lax.axis_index("ctx")
    chip, core = place // CORES, place % CORES
    last_group = chip >= edge
    chunks = [(which, head) for which in sides for head in range(Q_HEADS)]

    def mask_of(which, key_base):
        query_place = place if which == 0 else place + 1 - 2 * core
        query_pos = query_place * rows + lax.broadcasted_iota(jnp.int32, (1, rows), 1)
        low = jnp.zeros_like(query_pos)
        for number in range(starts_ref.shape[1]):
            start = starts_ref[:, number : number + 1]
            low = jnp.where(start <= query_pos, jnp.maximum(start, low), low)
        key_pos = key_base + lax.broadcasted_iota(jnp.int32, (rows, 1), 0)
        return (key_pos <= query_pos) & (key_pos >= low)

    def update(olds, chunks, parts):
        scores = []
        for which, head in chunks:
            queries = side_q[which][:, head * D_HEAD : (head + 1) * D_HEAD]
            row = []
            for block, masks in parts:
                s = lax.dot_general(block[0][...], queries, NT, preferred_element_type=jnp.float32)
                row.append(s if masks is None else jnp.where(masks[which], s, MASKED))
            scores.append(row)
        tops = []
        for (which, head), row in zip(chunks, scores):
            top = functools.reduce(jnp.maximum, [jnp.max(s, axis=0, keepdims=True) for s in row]) * FACTOR
            old_top = FLOOR if olds is None else olds[which][head, D_HEAD : D_HEAD + 1]
            tops.append((jnp.maximum(top, old_top), old_top))
        totals, expos = [], []
        for row, (top, _) in zip(scores, tops):
            row = [jnp.exp2(s * FACTOR - top) for s in row]
            totals.append(functools.reduce(jnp.add, [jnp.sum(expo, axis=0, keepdims=True) for expo in row]))
            expos.append([expo.astype(jnp.bfloat16) for expo in row])
        for (which, head), row, (top, old_top), total in zip(chunks, expos, tops, totals):
            weighted = functools.reduce(
                jnp.add,
                [
                    lax.dot_general(block[1][...], expo, TN, preferred_element_type=jnp.float32)
                    for expo, (block, _) in zip(row, parts)
                ],
            )
            if olds is not None:
                rescale = jnp.exp2(old_top - top)
                total = total + olds[which][head, D_HEAD + 1 : D_HEAD + 2] * rescale
                weighted = weighted + olds[which][head, :D_HEAD] * rescale
            news[which][head, :D_HEAD] = weighted
            news[which][head, D_HEAD : D_HEAD + 1] = top
            news[which][head, D_HEAD + 1 : D_HEAD + 2] = total

    received = []
    for table, block in zip(tables, blocks[len(blocks) - len(tables) :]):
        source = pick(chip, table)
        useful = (source < chip) & ((source >= edge) | (chip < edge))
        received.append((block, source, useful, any(entry < number for number, entry in enumerate(table[:edge]))))

    def one_by_one():
        for block, source, useful, early in received:

            @pl.when(useful & last_group)
            def _(block=block):
                update(news, chunks, [(block, None)])

            if early:

                @pl.when(useful & jnp.logical_not(last_group))
                def _(block=block, source=source):
                    base = (source * CORES + core) * rows
                    update(news, chunks, [(block, {which: mask_of(which, base) for which in sides})])

    if first:
        masks = {which: mask_of(which, place * rows) for which in sides}
        update(None, [chunk for chunk in chunks if chunk[0] == 0], [(blocks[0], masks)])

        @pl.when(core == 0)
        def _():
            update(None, [chunk for chunk in chunks if chunk[0] == 1], [(blocks[0], masks)])

        @pl.when(core == 1)
        def _():
            news[1][...] = jnp.zeros_like(news[1])
            news[1][:, D_HEAD : D_HEAD + 1] = jnp.full((Q_HEADS, 1, rows), FLOOR, jnp.float32)

        one_by_one()
    else:
        patterns = {tuple(edge <= table[chip] < chip for table in tables) for chip in range(edge, len(tables[0]))}
        joint = jnp.bool_(False)
        for pattern in sorted(patterns):
            if sum(pattern) < 2:
                continue
            here = last_group
            for wanted, (_, _, useful, _) in zip(pattern, received):
                here = here & (useful if wanted else jnp.logical_not(useful))
            joint = joint | here

            @pl.when(here)
            def _(pattern=pattern):
                update(olds, chunks, [(entry[0], None) for wanted, entry in zip(pattern, received) if wanted])

        @pl.when(jnp.logical_not(joint))
        def _():
            for which in sides:
                news[which][...] = olds[which][...]
            one_by_one()


def merge_kernel(own_ref, twin_ref, out_ref):
    for head in range(Q_HEADS):
        own_top, twin_top = own_ref[head, D_HEAD : D_HEAD + 1], twin_ref[head, D_HEAD : D_HEAD + 1]
        top = jnp.maximum(own_top, twin_top)
        own_scale, twin_scale = jnp.exp2(own_top - top), jnp.exp2(twin_top - top)
        total = (
            own_ref[head, D_HEAD + 1 : D_HEAD + 2] * own_scale + twin_ref[head, D_HEAD + 1 : D_HEAD + 2] * twin_scale
        )
        result = own_ref[head, :D_HEAD] * (own_scale / total) + twin_ref[head, :D_HEAD] * (twin_scale / total)
        out_ref[:, head * D_HEAD : (head + 1) * D_HEAD] = result.T.astype(jnp.bfloat16)


def vmem_call(kernel, out_shape, operands, flops):
    vmem = pl.BlockSpec(memory_space=pltpu.VMEM)
    return pl.pallas_call(
        kernel,
        out_shape=out_shape,
        in_specs=[vmem] * len(operands),
        out_specs=jax.tree.map(lambda _: vmem, out_shape),
        compiler_params=pltpu.CompilerParams(vmem_limit_bytes=32 * 1024 * 1024),
        cost_estimate=pl.CostEstimate(flops=flops, bytes_accessed=0, transcendentals=0),
    )(*operands)


def shards(count, queries, keys, values, doc_starts):
    chips = count // CORES
    plan = slots_of(chips)
    edge = chip_groups(chips)[-1][0]
    rows = queries.shape[0]
    swap = [(place, place + 1 - 2 * (place % CORES)) for place in range(count)]
    seen = useful_sources(plan)
    starts = doc_starts.reshape(1, -1)
    own = {True: (keys, values), False: (jnp.concatenate([keys, values], axis=1),)}
    arrived = []
    for operand, split, targets in plan:
        block = own[split] if operand is None else arrived[operand]
        arrived.append(tuple(lax.ppermute(part, "ctx", over_cores(targets)) for part in block))
    both = (queries, lax.ppermute(queries, "ctx", swap))
    partial = jax.ShapeDtypeStruct((Q_HEADS, D_HEAD + STAT_ROWS, rows), jnp.float32)
    stages = stages_of(chips, len(plan))
    state = ()
    for number, slots in enumerate(stages):
        blocks = ([] if state else [own[plan[0][1]]]) + [arrived[slot] for slot in slots]
        widths = [len(block) for block in blocks]
        tables = [seen[slot] for slot in slots]
        new = [None, None]
        for sides in [(1,), (0,)] if number == len(stages) - 1 and state else [(0, 1)]:
            flops = len(blocks) * len(sides) * Q_HEADS * rows * rows * D_HEAD * 4
            kernel = functools.partial(attend_kernel, tables, widths, not state, sides, edge)
            operands = [starts, *(both[side] for side in sides), *(part for block in blocks for part in block)]
            operands += [state[side] for side in sides] if state else []
            for side, result in zip(sides, vmem_call(kernel, (partial,) * len(sides), operands, flops)):
                new[side] = result
        state = tuple(new)
    mine, others = state
    out_shape = jax.ShapeDtypeStruct(queries.shape, jnp.bfloat16)
    return vmem_call(merge_kernel, out_shape, (mine, lax.ppermute(others, "ctx", swap)), 1000)


def solution(mesh):
    return jax.shard_map(
        functools.partial(shards, mesh.shape["ctx"]),
        mesh=mesh,
        in_specs=(P("ctx", "head"), P("ctx", "head"), P("ctx", "head"), P("head")),
        out_specs=P("ctx", "head"),
        check_vma=False,
    )
```

```python
import functools
import math

import jax
import jax.numpy as jnp
from jax import lax
from jax.experimental import pallas as pl
from jax.experimental.pallas import tpu as pltpu
from jax.sharding import PartitionSpec as P

D_HEAD = 128
Q_HEADS = 2
CORES = 2
STAT_ROWS = 8
PACKED_ROWS = 16
PIECES = 3
SCALE = 144.0 ** (-0.5)
FACTOR = SCALE * math.log2(math.e)
MASKED = -1e30
FLOOR = -1e29
NT = (((1,), (1,)), ((), ()))
TN = (((0,), (0,)), ((), ()))


def chip_groups(chips):
    if chips % 8 == 0:
        edge = 3 * chips // 8
        return ((0, edge), (edge, chips))
    return ((0, chips),)


def rotations(chips):
    groups = chip_groups(chips)
    steps = max(high - low for low, high in groups) - 1
    plan = []
    for step in range(steps, 0, -1):
        targets = [0] * chips
        for low, high in groups:
            size = high - low
            turn = step if step < size else 1 + step % (size - 1)
            for chip in range(low, high):
                targets[chip] = low + (chip - low + turn) % size
        plan.append((None, False, targets, None))
    return plan


def slots_of(chips):
    if chips == 8:
        return [
            (None, True, [1, 2, 0, 4, 6, 7, 3, 5], None),
            (None, False, [2, None, 0, 7, 5, 4, None, 3], None),
            (None, False, [None, None, None, 5, None, 3, 7, 6], None),
            (0, False, [None, None, None, None, None, None, 7, 6], None),
            (0, False, [None, None, None, None, 6, None, 4, None], None),
        ]
    return rotations(chips)


def stages_of(chips, count):
    if chips == 8:
        return [[0], [1], [2], [4], [3]]
    return [list(range(low, min(low + 4, count))) for low in range(0, count, 4)]


def over_cores(targets):
    return [
        (CORES * chip + core, CORES * chip + 1 - core if target is None else CORES * target + core)
        for chip, target in enumerate(targets)
        for core in range(CORES)
    ]


def useful_sources(plan):
    had, origins, tables = set(), [], []
    for operand, _, targets, _ in plan:
        origin = list(range(len(targets)))
        for chip, target in enumerate(targets):
            if target is not None:
                origin[target] = chip if operand is None else origins[operand][chip]
        origins.append(origin)
        tables.append(tuple(chip if (source, chip) in had else source for chip, source in enumerate(origin)))
        had.update((source, chip) for chip, source in enumerate(origin))
    for low, high in chip_groups(len(origins[0])):
        for chip in range(low, high):
            assert all((source, chip) in had for source in range(low, chip))
    return tables


def pick(index, table):
    runs = [(0, table[0])]
    for place in range(1, len(table)):
        if table[place] - place != runs[-1][1] - runs[-1][0]:
            runs.append((place, table[place]))
    value = index + (runs[0][1] - runs[0][0])
    for place, entry in runs[1:]:
        value = jnp.where(index >= place, index + (entry - place), value)
    return value


def pieces_of(row):
    pieces = []
    for _ in range(PIECES):
        pieces.append(row.astype(jnp.bfloat16))
        row = row - pieces[-1].astype(jnp.float32)
    return pieces


def attend_kernel(tables, widths, first, sides, edge, packed, *refs):
    refs = list(refs)
    if packed:
        work = refs.pop()
    starts_ref = refs.pop(0)
    side_q = {side: refs.pop(0) for side in sides}
    blocks = []
    for width in widths:
        parts = [refs.pop(0) for _ in range(width)]
        blocks.append((parts[0].at[:, :D_HEAD], parts[-1].at[:, (D_HEAD if width == 1 else 0) :]))
    olds = None if first else {side: refs.pop(0) for side in sides}
    outs = {side: refs.pop(0) for side in sides}
    news = {sides[0]: work} if packed else outs
    rows = side_q[sides[0]].shape[0]
    place = lax.axis_index("ctx")
    chip, core = place // CORES, place % CORES
    last_group = chip >= edge
    chunks = [(which, head) for which in sides for head in range(Q_HEADS)]

    def mask_of(which, key_base):
        query_place = place if which == 0 else place + 1 - 2 * core
        query_pos = query_place * rows + lax.broadcasted_iota(jnp.int32, (1, rows), 1)
        low = jnp.zeros_like(query_pos)
        for number in range(starts_ref.shape[1]):
            start = starts_ref[:, number : number + 1]
            low = jnp.where(start <= query_pos, jnp.maximum(start, low), low)
        key_pos = key_base + lax.broadcasted_iota(jnp.int32, (rows, 1), 0)
        return (key_pos <= query_pos) & (key_pos >= low)

    def update(olds, chunks, parts):
        scores = []
        for which, head in chunks:
            queries = side_q[which][:, head * D_HEAD : (head + 1) * D_HEAD]
            row = []
            for block, masks in parts:
                s = lax.dot_general(block[0][...], queries, NT, preferred_element_type=jnp.float32)
                row.append(s if masks is None else jnp.where(masks[which], s, MASKED))
            scores.append(row)
        tops = []
        for (which, head), row in zip(chunks, scores):
            top = functools.reduce(jnp.maximum, [jnp.max(s, axis=0, keepdims=True) for s in row]) * FACTOR
            old_top = FLOOR if olds is None else olds[which][head, D_HEAD : D_HEAD + 1]
            tops.append((jnp.maximum(top, old_top), old_top))
        totals, expos = [], []
        for row, (top, _) in zip(scores, tops):
            row = [jnp.exp2(s * FACTOR - top) for s in row]
            totals.append(functools.reduce(jnp.add, [jnp.sum(expo, axis=0, keepdims=True) for expo in row]))
            expos.append([expo.astype(jnp.bfloat16) for expo in row])
        for (which, head), row, (top, old_top), total in zip(chunks, expos, tops, totals):
            weighted = functools.reduce(
                jnp.add,
                [
                    lax.dot_general(block[1][...], expo, TN, preferred_element_type=jnp.float32)
                    for expo, (block, _) in zip(row, parts)
                ],
            )
            if olds is not None:
                rescale = jnp.exp2(old_top - top)
                total = total + olds[which][head, D_HEAD + 1 : D_HEAD + 2] * rescale
                weighted = weighted + olds[which][head, :D_HEAD] * rescale
            news[which][head, :D_HEAD] = weighted
            news[which][head, D_HEAD : D_HEAD + 1] = top
            news[which][head, D_HEAD + 1 : D_HEAD + 2] = total

    received = []
    for table, block in zip(tables, blocks[len(blocks) - len(tables) :]):
        source = pick(chip, table)
        useful = (source < chip) & ((source >= edge) | (chip < edge))
        received.append((block, source, useful, any(entry < number for number, entry in enumerate(table[:edge]))))

    def one_by_one():
        for block, source, useful, early in received:

            @pl.when(useful & last_group)
            def _(block=block):
                update(news, chunks, [(block, None)])

            if early:

                @pl.when(useful & jnp.logical_not(last_group))
                def _(block=block, source=source):
                    base = (source * CORES + core) * rows
                    update(news, chunks, [(block, {which: mask_of(which, base) for which in sides})])

    if first:
        masks = {which: mask_of(which, place * rows) for which in sides}
        update(None, [chunk for chunk in chunks if chunk[0] == 0], [(blocks[0], masks)])

        @pl.when(core == 0)
        def _():
            update(None, [chunk for chunk in chunks if chunk[0] == 1], [(blocks[0], masks)])

        @pl.when(core == 1)
        def _():
            news[1][...] = jnp.zeros_like(news[1])
            news[1][:, D_HEAD : D_HEAD + 1] = jnp.full((Q_HEADS, 1, rows), FLOOR, jnp.float32)

        one_by_one()
    else:
        patterns = {tuple(edge <= table[chip] < chip for table in tables) for chip in range(edge, len(tables[0]))}
        joint = jnp.bool_(False)
        for pattern in sorted(patterns):
            if sum(pattern) < 2:
                continue
            here = last_group
            for wanted, (_, _, useful, _) in zip(pattern, received):
                here = here & (useful if wanted else jnp.logical_not(useful))
            joint = joint | here

            @pl.when(here)
            def _(pattern=pattern):
                update(olds, chunks, [(entry[0], None) for wanted, entry in zip(pattern, received) if wanted])

        @pl.when(jnp.logical_not(joint))
        def _():
            for which in sides:
                news[which][...] = olds[which][...]
            one_by_one()

    if packed:
        for head in range(Q_HEADS):
            low = []
            for row in (D_HEAD, D_HEAD + 1):
                low += pieces_of(work[head, row : row + 1])
            low.append(jnp.zeros((PACKED_ROWS - 2 * PIECES, rows), jnp.bfloat16))
            outs[sides[0]][head, :D_HEAD] = work[head, :D_HEAD].astype(jnp.bfloat16)
            outs[sides[0]][head, D_HEAD:] = jnp.concatenate(low, axis=0)


def merge_kernel(own_ref, twin_ref, out_ref):
    for head in range(Q_HEADS):
        low = twin_ref[head, D_HEAD:].astype(jnp.float32)
        rows_of = [low[number : number + 1] for number in range(2 * PIECES)]
        twin_top = functools.reduce(jnp.add, rows_of[:PIECES])
        twin_total = functools.reduce(jnp.add, rows_of[PIECES:])
        own_top = own_ref[head, D_HEAD : D_HEAD + 1]
        top = jnp.maximum(own_top, twin_top)
        own_scale, twin_scale = jnp.exp2(own_top - top), jnp.exp2(twin_top - top)
        total = own_ref[head, D_HEAD + 1 : D_HEAD + 2] * own_scale + twin_total * twin_scale
        twin = twin_ref[head, :D_HEAD].astype(jnp.float32)
        result = own_ref[head, :D_HEAD] * (own_scale / total) + twin * (twin_scale / total)
        out_ref[:, head * D_HEAD : (head + 1) * D_HEAD] = result.T.astype(jnp.bfloat16)


def vmem_call(kernel, out_shape, operands, flops, scratch=()):
    vmem = pl.BlockSpec(memory_space=pltpu.VMEM)
    return pl.pallas_call(
        kernel,
        out_shape=out_shape,
        in_specs=[vmem] * len(operands),
        out_specs=jax.tree.map(lambda _: vmem, out_shape),
        scratch_shapes=scratch,
        compiler_params=pltpu.CompilerParams(vmem_limit_bytes=32 * 1024 * 1024),
        cost_estimate=pl.CostEstimate(flops=flops, bytes_accessed=0, transcendentals=0),
    )(*operands)


def shards(count, queries, keys, values, doc_starts):
    chips = count // CORES
    plan = slots_of(chips)
    edge = chip_groups(chips)[-1][0]
    rows = queries.shape[0]
    swap = [(place, place + 1 - 2 * (place % CORES)) for place in range(count)]
    seen = useful_sources(plan)
    starts = doc_starts.reshape(1, -1)
    own = {True: (keys, values), False: (jnp.concatenate([keys, values], axis=1),)}
    arrived = []
    for operand, split, targets, after in plan:
        block = own[split] if operand is None else arrived[operand]
        if len(block) > 1 and not split:
            block = (jnp.concatenate(block, axis=1),)
        if after is not None:
            block = lax.optimization_barrier((*block, *arrived[after]))[: len(block)]
        arrived.append(tuple(lax.ppermute(part, "ctx", over_cores(targets)) for part in block))
    both = (queries, lax.ppermute(queries, "ctx", swap))
    partial = jax.ShapeDtypeStruct((Q_HEADS, D_HEAD + STAT_ROWS, rows), jnp.float32)
    to_send = jax.ShapeDtypeStruct((Q_HEADS, D_HEAD + PACKED_ROWS, rows), jnp.bfloat16)
    stages = stages_of(chips, len(plan))
    state = ()
    for number, slots in enumerate(stages):
        blocks = ([] if state else [own[plan[0][1]]]) + [arrived[slot] for slot in slots]
        widths = [len(block) for block in blocks]
        tables = [seen[slot] for slot in slots]
        new = [None, None]
        last = number == len(stages) - 1
        for sides in [(1,), (0,)] if last and state else [(0, 1)]:
            flops = len(blocks) * len(sides) * Q_HEADS * rows * rows * D_HEAD * 4
            packed = last and sides == (1,)
            kernel = functools.partial(attend_kernel, tables, widths, not state, sides, edge, packed)
            operands = [starts, *(both[side] for side in sides), *(part for block in blocks for part in block)]
            operands += [state[side] for side in sides] if state else []
            out_shape = (to_send if packed else partial,) * len(sides)
            scratch = [pltpu.VMEM(partial.shape, partial.dtype)] if packed else []
            for side, result in zip(sides, vmem_call(kernel, out_shape, operands, flops, scratch)):
                new[side] = result
        state = tuple(new)
    mine, others = state
    out_shape = jax.ShapeDtypeStruct(queries.shape, jnp.bfloat16)
    return vmem_call(merge_kernel, out_shape, (mine, lax.ppermute(others, "ctx", swap)), 1000)


def solution(mesh):
    return jax.shard_map(
        functools.partial(shards, mesh.shape["ctx"]),
        mesh=mesh,
        in_specs=(P("ctx", "head"), P("ctx", "head"), P("ctx", "head"), P("head")),
        out_specs=P("ctx", "head"),
        check_vma=False,
    )
```

```python
import functools
import math

import jax
import jax.numpy as jnp
from jax import lax
from jax.experimental import pallas as pl
from jax.experimental.pallas import tpu as pltpu
from jax.sharding import PartitionSpec as P

D_HEAD = 128
Q_HEADS = 2
CORES = 2
STAT_ROWS = 8
PACKED_ROWS = 16
PIECES = 3
SCALE = 144.0 ** (-0.5)
FACTOR = SCALE * math.log2(math.e)
MASKED = -1e30
FLOOR = -1e29
NT = (((1,), (1,)), ((), ()))
TN = (((0,), (0,)), ((), ()))


def chip_groups(chips):
    if chips % 8 == 0:
        edge = 3 * chips // 8
        return ((0, edge), (edge, chips))
    return ((0, chips),)


def rotations(chips):
    groups = chip_groups(chips)
    steps = max(high - low for low, high in groups) - 1
    plan = []
    for step in range(steps, 0, -1):
        targets = [0] * chips
        for low, high in groups:
            size = high - low
            turn = step if step < size else 1 + step % (size - 1)
            for chip in range(low, high):
                targets[chip] = low + (chip - low + turn) % size
        plan.append((None, False, targets, None))
    return plan


def slots_of(chips):
    if chips == 8:
        return [
            (None, True, [1, 2, 0, 4, 6, 7, 3, 5], None),
            (None, False, [2, None, 0, 7, 5, 4, None, 3], None),
            (None, False, [None, None, None, 5, None, 3, 7, 6], None),
            (0, False, [None, None, None, None, None, None, 7, 6], None),
            (0, False, [None, None, None, None, 6, None, 4, None], None),
        ]
    return rotations(chips)


def stages_of(chips, count):
    if chips == 8:
        return [[0], [1], [2], [4], [3]]
    return [list(range(low, min(low + 4, count))) for low in range(0, count, 4)]


def over_cores(targets):
    return [
        (CORES * chip + core, CORES * chip + 1 - core if target is None else CORES * target + core)
        for chip, target in enumerate(targets)
        for core in range(CORES)
    ]


def useful_sources(plan):
    had, origins, tables = set(), [], []
    for operand, _, targets, _ in plan:
        origin = list(range(len(targets)))
        for chip, target in enumerate(targets):
            if target is not None:
                origin[target] = chip if operand is None else origins[operand][chip]
        origins.append(origin)
        tables.append(tuple(chip if (source, chip) in had else source for chip, source in enumerate(origin)))
        had.update((source, chip) for chip, source in enumerate(origin))
    for low, high in chip_groups(len(origins[0])):
        for chip in range(low, high):
            assert all((source, chip) in had for source in range(low, chip))
    return tables


def pick(index, table):
    runs = [(0, table[0])]
    for place in range(1, len(table)):
        if table[place] - place != runs[-1][1] - runs[-1][0]:
            runs.append((place, table[place]))
    value = index + (runs[0][1] - runs[0][0])
    for place, entry in runs[1:]:
        value = jnp.where(index >= place, index + (entry - place), value)
    return value


def pieces_of(row):
    pieces = []
    for _ in range(PIECES):
        pieces.append(row.astype(jnp.bfloat16))
        row = row - pieces[-1].astype(jnp.float32)
    return pieces


def attend_kernel(tables, widths, first, sides, edge, packed, *refs):
    refs = list(refs)
    if packed:
        work = refs.pop()
    starts_ref = refs.pop(0)
    side_q = {side: refs.pop(0) for side in sides}
    blocks = []
    for width in widths:
        parts = [refs.pop(0) for _ in range(width)]
        blocks.append((parts[0].at[:, :D_HEAD], parts[-1].at[:, (D_HEAD if width == 1 else 0) :]))
    olds = None if first else {side: refs.pop(0) for side in sides}
    outs = {side: refs.pop(0) for side in sides}
    news = {sides[0]: work} if packed else outs
    rows = side_q[sides[0]].shape[0]
    place = lax.axis_index("ctx")
    chip, core = place // CORES, place % CORES
    last_group = chip >= edge
    chunks = [(which, head) for which in sides for head in range(Q_HEADS)]

    def mask_of(which, key_base):
        query_place = place if which == 0 else place + 1 - 2 * core
        query_pos = query_place * rows + lax.broadcasted_iota(jnp.int32, (1, rows), 1)
        low = jnp.zeros_like(query_pos)
        for number in range(starts_ref.shape[1]):
            start = starts_ref[:, number : number + 1]
            low = jnp.where(start <= query_pos, jnp.maximum(start, low), low)
        key_pos = key_base + lax.broadcasted_iota(jnp.int32, (rows, 1), 0)
        return (key_pos <= query_pos) & (key_pos >= low)

    def update(olds, chunks, parts):
        scores = []
        for which, head in chunks:
            queries = side_q[which][:, head * D_HEAD : (head + 1) * D_HEAD]
            row = []
            for block, masks in parts:
                s = lax.dot_general(block[0][...], queries, NT, preferred_element_type=jnp.float32)
                row.append(s if masks is None else jnp.where(masks[which], s, MASKED))
            scores.append(row)
        tops = []
        for (which, head), row in zip(chunks, scores):
            top = functools.reduce(jnp.maximum, [jnp.max(s, axis=0, keepdims=True) for s in row]) * FACTOR
            old_top = FLOOR if olds is None else olds[which][head, D_HEAD : D_HEAD + 1]
            tops.append((jnp.maximum(top, old_top), old_top))
        totals, expos = [], []
        for row, (top, _) in zip(scores, tops):
            row = [jnp.exp2(s * FACTOR - top) for s in row]
            totals.append(functools.reduce(jnp.add, [jnp.sum(expo, axis=0, keepdims=True) for expo in row]))
            expos.append([expo.astype(jnp.bfloat16) for expo in row])
        for (which, head), row, (top, old_top), total in zip(chunks, expos, tops, totals):
            weighted = functools.reduce(
                jnp.add,
                [
                    lax.dot_general(block[1][...], expo, TN, preferred_element_type=jnp.float32)
                    for expo, (block, _) in zip(row, parts)
                ],
            )
            if olds is not None:
                rescale = jnp.exp2(old_top - top)
                total = total + olds[which][head, D_HEAD + 1 : D_HEAD + 2] * rescale
                weighted = weighted + olds[which][head, :D_HEAD] * rescale
            news[which][head, :D_HEAD] = weighted
            news[which][head, D_HEAD : D_HEAD + 1] = top
            news[which][head, D_HEAD + 1 : D_HEAD + 2] = total

    received = []
    for table, block in zip(tables, blocks[len(blocks) - len(tables) :]):
        source = pick(chip, table)
        useful = (source < chip) & ((source >= edge) | (chip < edge))
        received.append((block, source, useful, any(entry < number for number, entry in enumerate(table[:edge]))))

    def one_by_one():
        for block, source, useful, early in received:

            @pl.when(useful & last_group)
            def _(block=block):
                update(news, chunks, [(block, None)])

            if early:

                @pl.when(useful & jnp.logical_not(last_group))
                def _(block=block, source=source):
                    base = (source * CORES + core) * rows
                    update(news, chunks, [(block, {which: mask_of(which, base) for which in sides})])

    if first:
        masks = {which: mask_of(which, place * rows) for which in sides}
        update(None, [chunk for chunk in chunks if chunk[0] == 0], [(blocks[0], masks)])

        @pl.when(core == 0)
        def _():
            update(None, [chunk for chunk in chunks if chunk[0] == 1], [(blocks[0], masks)])

        @pl.when(core == 1)
        def _():
            news[1][...] = jnp.zeros_like(news[1])
            news[1][:, D_HEAD : D_HEAD + 1] = jnp.full((Q_HEADS, 1, rows), FLOOR, jnp.float32)

        one_by_one()
    else:
        patterns = {tuple(edge <= table[chip] < chip for table in tables) for chip in range(edge, len(tables[0]))}
        joint = jnp.bool_(False)
        for pattern in sorted(patterns):
            if sum(pattern) < 1:
                continue
            here = last_group
            for wanted, (_, _, useful, _) in zip(pattern, received):
                here = here & (useful if wanted else jnp.logical_not(useful))
            joint = joint | here

            @pl.when(here)
            def _(pattern=pattern):
                update(olds, chunks, [(entry[0], None) for wanted, entry in zip(pattern, received) if wanted])

        @pl.when(jnp.logical_not(joint))
        def _():
            for which in sides:
                news[which][...] = olds[which][...]
            one_by_one()

    if packed:
        for head in range(Q_HEADS):
            low = []
            for row in (D_HEAD, D_HEAD + 1):
                low += pieces_of(work[head, row : row + 1])
            low.append(jnp.zeros((PACKED_ROWS - 2 * PIECES, rows), jnp.bfloat16))
            outs[sides[0]][head, :D_HEAD] = work[head, :D_HEAD].astype(jnp.bfloat16)
            outs[sides[0]][head, D_HEAD:] = jnp.concatenate(low, axis=0)


def merge_kernel(own_ref, twin_ref, out_ref):
    for head in range(Q_HEADS):
        low = twin_ref[head, D_HEAD:].astype(jnp.float32)
        rows_of = [low[number : number + 1] for number in range(2 * PIECES)]
        twin_top = functools.reduce(jnp.add, rows_of[:PIECES])
        twin_total = functools.reduce(jnp.add, rows_of[PIECES:])
        own_top = own_ref[head, D_HEAD : D_HEAD + 1]
        top = jnp.maximum(own_top, twin_top)
        own_scale, twin_scale = jnp.exp2(own_top - top), jnp.exp2(twin_top - top)
        total = own_ref[head, D_HEAD + 1 : D_HEAD + 2] * own_scale + twin_total * twin_scale
        twin = twin_ref[head, :D_HEAD].astype(jnp.float32)
        result = own_ref[head, :D_HEAD] * (own_scale / total) + twin * (twin_scale / total)
        out_ref[:, head * D_HEAD : (head + 1) * D_HEAD] = result.T.astype(jnp.bfloat16)


def vmem_call(kernel, out_shape, operands, flops, scratch=()):
    vmem = pl.BlockSpec(memory_space=pltpu.VMEM)
    return pl.pallas_call(
        kernel,
        out_shape=out_shape,
        in_specs=[vmem] * len(operands),
        out_specs=jax.tree.map(lambda _: vmem, out_shape),
        scratch_shapes=scratch,
        compiler_params=pltpu.CompilerParams(vmem_limit_bytes=32 * 1024 * 1024),
        cost_estimate=pl.CostEstimate(flops=flops, bytes_accessed=0, transcendentals=0),
    )(*operands)


def shards(count, queries, keys, values, doc_starts):
    chips = count // CORES
    plan = slots_of(chips)
    edge = chip_groups(chips)[-1][0]
    rows = queries.shape[0]
    swap = [(place, place + 1 - 2 * (place % CORES)) for place in range(count)]
    seen = useful_sources(plan)
    starts = doc_starts.reshape(1, -1)
    own = {True: (keys, values), False: (jnp.concatenate([keys, values], axis=1),)}
    arrived = []
    for operand, split, targets, after in plan:
        block = own[split] if operand is None else arrived[operand]
        if len(block) > 1 and not split:
            block = (jnp.concatenate(block, axis=1),)
        if after is not None:
            block = lax.optimization_barrier((*block, *arrived[after]))[: len(block)]
        arrived.append(tuple(lax.ppermute(part, "ctx", over_cores(targets)) for part in block))
    both = (queries, lax.ppermute(queries, "ctx", swap))
    partial = jax.ShapeDtypeStruct((Q_HEADS, D_HEAD + STAT_ROWS, rows), jnp.float32)
    to_send = jax.ShapeDtypeStruct((Q_HEADS, D_HEAD + PACKED_ROWS, rows), jnp.bfloat16)
    stages = stages_of(chips, len(plan))
    state = ()
    for number, slots in enumerate(stages):
        blocks = ([] if state else [own[plan[0][1]]]) + [arrived[slot] for slot in slots]
        widths = [len(block) for block in blocks]
        tables = [seen[slot] for slot in slots]
        new = [None, None]
        last = number == len(stages) - 1
        for sides in [(1,), (0,)] if last and state else [(0, 1)]:
            flops = len(blocks) * len(sides) * Q_HEADS * rows * rows * D_HEAD * 4
            packed = last and sides == (1,)
            kernel = functools.partial(attend_kernel, tables, widths, not state, sides, edge, packed)
            operands = [starts, *(both[side] for side in sides), *(part for block in blocks for part in block)]
            operands += [state[side] for side in sides] if state else []
            out_shape = (to_send if packed else partial,) * len(sides)
            scratch = [pltpu.VMEM(partial.shape, partial.dtype)] if packed else []
            for side, result in zip(sides, vmem_call(kernel, out_shape, operands, flops, scratch)):
                new[side] = result
        state = tuple(new)
    mine, others = state
    out_shape = jax.ShapeDtypeStruct(queries.shape, jnp.bfloat16)
    return vmem_call(merge_kernel, out_shape, (mine, lax.ppermute(others, "ctx", swap)), 1000)


def solution(mesh):
    return jax.shard_map(
        functools.partial(shards, mesh.shape["ctx"]),
        mesh=mesh,
        in_specs=(P("ctx", "head"), P("ctx", "head"), P("ctx", "head"), P("head")),
        out_specs=P("ctx", "head"),
        check_vma=False,
    )
```

```python
import functools
import math

import jax
import jax.numpy as jnp
from jax import lax
from jax.experimental import pallas as pl
from jax.experimental.pallas import tpu as pltpu
from jax.sharding import PartitionSpec as P

D_HEAD = 128
Q_HEADS = 2
CORES = 2
STAT_ROWS = 8
PACKED_ROWS = 16
PIECES = 3
SCALE = 144.0 ** (-0.5)
FACTOR = SCALE * math.log2(math.e)
MASKED = -1e30
FLOOR = -1e29
NT = (((1,), (1,)), ((), ()))
TN = (((0,), (0,)), ((), ()))


def chip_groups(chips):
    if chips % 8 == 0:
        edge = 3 * chips // 8
        return ((0, edge), (edge, chips))
    return ((0, chips),)


def rotations(chips):
    groups = chip_groups(chips)
    steps = max(high - low for low, high in groups) - 1
    plan = []
    for step in range(steps, 0, -1):
        targets = [0] * chips
        for low, high in groups:
            size = high - low
            turn = step if step < size else 1 + step % (size - 1)
            for chip in range(low, high):
                targets[chip] = low + (chip - low + turn) % size
        plan.append((None, False, targets, None))
    return plan


def slots_of(chips):
    if chips == 8:
        return [
            (None, False, [1, 2, 0, 4, 6, 7, 3, 5], None),
            (None, False, [2, None, 0, 6, 5, 4, 7, 3], None),
            (None, False, [None, None, None, 7, None, None, None, 3], None),
            (0, False, [None, None, None, None, 5, 4, 7, 6], None),
        ]
    return rotations(chips)


def stages_of(chips, count):
    if chips == 8:
        return [[0], [1], [2, 3]]
    return [list(range(low, min(low + 4, count))) for low in range(0, count, 4)]


def over_cores(targets):
    return [
        (CORES * chip + core, CORES * chip + 1 - core if target is None else CORES * target + core)
        for chip, target in enumerate(targets)
        for core in range(CORES)
    ]


def useful_sources(plan):
    had, origins, tables = set(), [], []
    for operand, _, targets, _ in plan:
        origin = list(range(len(targets)))
        for chip, target in enumerate(targets):
            if target is not None:
                origin[target] = chip if operand is None else origins[operand][chip]
        origins.append(origin)
        tables.append(tuple(chip if (source, chip) in had else source for chip, source in enumerate(origin)))
        had.update((source, chip) for chip, source in enumerate(origin))
    for low, high in chip_groups(len(origins[0])):
        for chip in range(low, high):
            assert all((source, chip) in had for source in range(low, chip))
    return tables


def pick(index, table):
    runs = [(0, table[0])]
    for place in range(1, len(table)):
        if table[place] - place != runs[-1][1] - runs[-1][0]:
            runs.append((place, table[place]))
    value = index + (runs[0][1] - runs[0][0])
    for place, entry in runs[1:]:
        value = jnp.where(index >= place, index + (entry - place), value)
    return value


def pieces_of(row):
    pieces = []
    for _ in range(PIECES):
        pieces.append(row.astype(jnp.bfloat16))
        row = row - pieces[-1].astype(jnp.float32)
    return pieces


def attend_kernel(tables, widths, first, sides, edge, packed, *refs):
    refs = list(refs)
    if packed:
        work = refs.pop()
    starts_ref = refs.pop(0)
    side_q = {side: refs.pop(0) for side in sides}
    blocks = []
    for width in widths:
        parts = [refs.pop(0) for _ in range(width)]
        blocks.append((parts[0].at[:, :D_HEAD], parts[-1].at[:, (D_HEAD if width == 1 else 0) :]))
    olds = None if first else {side: refs.pop(0) for side in sides}
    outs = {side: refs.pop(0) for side in sides}
    news = {sides[0]: work} if packed else outs
    rows = side_q[sides[0]].shape[0]
    place = lax.axis_index("ctx")
    chip, core = place // CORES, place % CORES
    last_group = chip >= edge
    chunks = [(which, head) for which in sides for head in range(Q_HEADS)]

    def mask_of(which, key_base):
        query_place = place if which == 0 else place + 1 - 2 * core
        query_pos = query_place * rows + lax.broadcasted_iota(jnp.int32, (1, rows), 1)
        low = jnp.zeros_like(query_pos)
        for number in range(starts_ref.shape[1]):
            start = starts_ref[:, number : number + 1]
            low = jnp.where(start <= query_pos, jnp.maximum(start, low), low)
        key_pos = key_base + lax.broadcasted_iota(jnp.int32, (rows, 1), 0)
        return (key_pos <= query_pos) & (key_pos >= low)

    def update(olds, chunks, parts):
        scores = []
        for which, head in chunks:
            queries = side_q[which][:, head * D_HEAD : (head + 1) * D_HEAD]
            row = []
            for block, masks in parts:
                s = lax.dot_general(block[0][...], queries, NT, preferred_element_type=jnp.float32)
                row.append(s if masks is None else jnp.where(masks[which], s, MASKED))
            scores.append(row)
        tops = []
        for (which, head), row in zip(chunks, scores):
            top = functools.reduce(jnp.maximum, [jnp.max(s, axis=0, keepdims=True) for s in row]) * FACTOR
            old_top = FLOOR if olds is None else olds[which][head, D_HEAD : D_HEAD + 1]
            tops.append((jnp.maximum(top, old_top), old_top))
        totals, expos = [], []
        for row, (top, _) in zip(scores, tops):
            row = [jnp.exp2(s * FACTOR - top) for s in row]
            totals.append(functools.reduce(jnp.add, [jnp.sum(expo, axis=0, keepdims=True) for expo in row]))
            expos.append([expo.astype(jnp.bfloat16) for expo in row])
        for (which, head), row, (top, old_top), total in zip(chunks, expos, tops, totals):
            weighted = functools.reduce(
                jnp.add,
                [
                    lax.dot_general(block[1][...], expo, TN, preferred_element_type=jnp.float32)
                    for expo, (block, _) in zip(row, parts)
                ],
            )
            if olds is not None:
                rescale = jnp.exp2(old_top - top)
                total = total + olds[which][head, D_HEAD + 1 : D_HEAD + 2] * rescale
                weighted = weighted + olds[which][head, :D_HEAD] * rescale
            news[which][head, :D_HEAD] = weighted
            news[which][head, D_HEAD : D_HEAD + 1] = top
            news[which][head, D_HEAD + 1 : D_HEAD + 2] = total

    received = []
    for table, block in zip(tables, blocks[len(blocks) - len(tables) :]):
        source = pick(chip, table)
        useful = (source < chip) & ((source >= edge) | (chip < edge))
        received.append((block, source, useful, any(entry < number for number, entry in enumerate(table[:edge]))))

    def one_by_one():
        for block, source, useful, early in received:

            @pl.when(useful & last_group)
            def _(block=block):
                update(news, chunks, [(block, None)])

            if early:

                @pl.when(useful & jnp.logical_not(last_group))
                def _(block=block, source=source):
                    base = (source * CORES + core) * rows
                    update(news, chunks, [(block, {which: mask_of(which, base) for which in sides})])

    if first:
        masks = {which: mask_of(which, place * rows) for which in sides}
        update(None, [chunk for chunk in chunks if chunk[0] == 0], [(blocks[0], masks)])

        @pl.when(core == 0)
        def _():
            update(None, [chunk for chunk in chunks if chunk[0] == 1], [(blocks[0], masks)])

        @pl.when(core == 1)
        def _():
            news[1][...] = jnp.zeros_like(news[1])
            news[1][:, D_HEAD : D_HEAD + 1] = jnp.full((Q_HEADS, 1, rows), FLOOR, jnp.float32)

        one_by_one()
    else:
        patterns = {tuple(edge <= table[chip] < chip for table in tables) for chip in range(edge, len(tables[0]))}
        joint = jnp.bool_(False)
        for pattern in sorted(patterns):
            if sum(pattern) < 1:
                continue
            here = last_group
            for wanted, (_, _, useful, _) in zip(pattern, received):
                here = here & (useful if wanted else jnp.logical_not(useful))
            joint = joint | here

            @pl.when(here)
            def _(pattern=pattern):
                update(olds, chunks, [(entry[0], None) for wanted, entry in zip(pattern, received) if wanted])

        @pl.when(jnp.logical_not(joint))
        def _():
            for which in sides:
                news[which][...] = olds[which][...]
            one_by_one()

    if packed:
        for head in range(Q_HEADS):
            low = []
            for row in (D_HEAD, D_HEAD + 1):
                low += pieces_of(work[head, row : row + 1])
            low.append(jnp.zeros((PACKED_ROWS - 2 * PIECES, rows), jnp.bfloat16))
            outs[sides[0]][head, :D_HEAD] = work[head, :D_HEAD].astype(jnp.bfloat16)
            outs[sides[0]][head, D_HEAD:] = jnp.concatenate(low, axis=0)


def merge_kernel(own_ref, twin_ref, out_ref):
    for head in range(Q_HEADS):
        low = twin_ref[head, D_HEAD:].astype(jnp.float32)
        rows_of = [low[number : number + 1] for number in range(2 * PIECES)]
        twin_top = functools.reduce(jnp.add, rows_of[:PIECES])
        twin_total = functools.reduce(jnp.add, rows_of[PIECES:])
        own_top = own_ref[head, D_HEAD : D_HEAD + 1]
        top = jnp.maximum(own_top, twin_top)
        own_scale, twin_scale = jnp.exp2(own_top - top), jnp.exp2(twin_top - top)
        total = own_ref[head, D_HEAD + 1 : D_HEAD + 2] * own_scale + twin_total * twin_scale
        twin = twin_ref[head, :D_HEAD].astype(jnp.float32)
        result = own_ref[head, :D_HEAD] * (own_scale / total) + twin * (twin_scale / total)
        out_ref[:, head * D_HEAD : (head + 1) * D_HEAD] = result.T.astype(jnp.bfloat16)


def vmem_call(kernel, out_shape, operands, flops, scratch=()):
    vmem = pl.BlockSpec(memory_space=pltpu.VMEM)
    return pl.pallas_call(
        kernel,
        out_shape=out_shape,
        in_specs=[vmem] * len(operands),
        out_specs=jax.tree.map(lambda _: vmem, out_shape),
        scratch_shapes=scratch,
        compiler_params=pltpu.CompilerParams(vmem_limit_bytes=32 * 1024 * 1024),
        cost_estimate=pl.CostEstimate(flops=flops, bytes_accessed=0, transcendentals=0),
    )(*operands)


def shards(count, queries, keys, values, doc_starts):
    chips = count // CORES
    plan = slots_of(chips)
    edge = chip_groups(chips)[-1][0]
    rows = queries.shape[0]
    swap = [(place, place + 1 - 2 * (place % CORES)) for place in range(count)]
    seen = useful_sources(plan)
    starts = doc_starts.reshape(1, -1)
    own = {True: (keys, values), False: (jnp.concatenate([keys, values], axis=1),)}
    arrived = []
    for operand, split, targets, after in plan:
        block = own[split] if operand is None else arrived[operand]
        if len(block) > 1 and not split:
            block = (jnp.concatenate(block, axis=1),)
        if after is not None:
            block = lax.optimization_barrier((*block, *arrived[after]))[: len(block)]
        arrived.append(tuple(lax.ppermute(part, "ctx", over_cores(targets)) for part in block))
    both = (queries, lax.ppermute(queries, "ctx", swap))
    partial = jax.ShapeDtypeStruct((Q_HEADS, D_HEAD + STAT_ROWS, rows), jnp.float32)
    to_send = jax.ShapeDtypeStruct((Q_HEADS, D_HEAD + PACKED_ROWS, rows), jnp.bfloat16)
    stages = stages_of(chips, len(plan))
    state = ()
    for number, slots in enumerate(stages):
        blocks = ([] if state else [own[plan[0][1]]]) + [arrived[slot] for slot in slots]
        widths = [len(block) for block in blocks]
        tables = [seen[slot] for slot in slots]
        new = [None, None]
        last = number == len(stages) - 1
        for sides in [(1,), (0,)] if last and state else [(0, 1)]:
            flops = len(blocks) * len(sides) * Q_HEADS * rows * rows * D_HEAD * 4
            packed = last and sides == (1,)
            kernel = functools.partial(attend_kernel, tables, widths, not state, sides, edge, packed)
            operands = [starts, *(both[side] for side in sides), *(part for block in blocks for part in block)]
            operands += [state[side] for side in sides] if state else []
            out_shape = (to_send if packed else partial,) * len(sides)
            scratch = [pltpu.VMEM(partial.shape, partial.dtype)] if packed else []
            for side, result in zip(sides, vmem_call(kernel, out_shape, operands, flops, scratch)):
                new[side] = result
        state = tuple(new)
    mine, others = state
    out_shape = jax.ShapeDtypeStruct(queries.shape, jnp.bfloat16)
    return vmem_call(merge_kernel, out_shape, (mine, lax.ppermute(others, "ctx", swap)), 1000)


def solution(mesh):
    return jax.shard_map(
        functools.partial(shards, mesh.shape["ctx"]),
        mesh=mesh,
        in_specs=(P("ctx", "head"), P("ctx", "head"), P("ctx", "head"), P("head")),
        out_specs=P("ctx", "head"),
        check_vma=False,
    )
```
